256 devices in a mesh: rows: 4 (over y_hi, core), cols: 64 (over y_lo, x, z).
Axes of the slice: x: 4, y: 4 (y_hi: 2, y_lo: 2; y = y_hi * 2 + y_lo), z: 8, core: 2. Of those that a mesh axis runs over, the one named last changes fastest.
Arguments:
- features: bfloat16 [128, 8192, 384], P('rows', 'cols'), may hold values from -6 to 6
- depth_weight: float32 [7, 7, 384], replicated, may hold values from -0.875 to 0.875
- depth_bias: float32 [384], replicated, may hold values from -3 to 3
- norm_gain: float32 [384], replicated, may hold values from 0.1 to 1.9
- norm_shift: float32 [384], replicated, may hold values from -2 to 2
- expand_weight: bfloat16 [384, 1536], replicated, may hold values from -0.3125 to 0.3125
- expand_bias: float32 [1536], replicated, may hold values from -3 to 3
- reduce_weight: bfloat16 [1536, 384], replicated, may hold values from -0.15625 to 0.15625
- reduce_bias: float32 [384], replicated, may hold values from -3 to 3
- layer_scale: float32 [384], replicated, may hold values from 0.3 to 1.5
- down_gain: float32 [384], replicated, may hold values from 0.1 to 1.9
- down_shift: float32 [384], replicated, may hold values from -2 to 2
- down_weight: bfloat16 [2, 2, 384, 768], replicated, may hold values from -0.15625 to 0.15625
- down_bias: float32 [768], replicated, may hold values from -3 to 3
Outputs:
- next_section: bfloat16 [64, 4096, 768], P(None, 'cols', 'rows')
The draws below stay inside these ranges and needn't reach their ends.
All inputs are finite; a program needn't handle non-finite values.
Results may differ from the reference program's by a relative error of at most 0.0059.
Values may be sent and summed in bfloat16 or wider, within the bound.
A program may use at most 128 MiB of HBM per device.

```python
import math
import jax
import jax.numpy as jnp
from jax import lax

C = 384
HID = 1536
C2 = 768
H = 128
W = 8192
H2 = 64
W2 = 4096


def block_scale(own_key, shape, pieces, low, high):
    level = 1.0
    for axis_at, parts in pieces:
        heights = jax.random.uniform(jax.random.fold_in(jax.random.fold_in(own_key, 6), axis_at), (parts,), jnp.float32, low / len(pieces), high / len(pieces))
        level = level * jnp.repeat(jnp.exp(heights), shape[axis_at] // parts).reshape((-1,) + (1,) * (len(shape) - 1 - axis_at))
    return level


def bell_draw(rng, shape, scale, most, split=(), kind=jnp.bfloat16):
    factor_of = block_scale(rng, shape, split, -0.22, 0.18) if split else 1.0
    values = jax.random.normal(rng, shape, jnp.float32) * scale * factor_of
    return jnp.minimum(jnp.maximum(values, -most), most).astype(kind)


def setup_inputs(seed: int = 0) -> dict:
    splits = jax.random.split(jax.random.key(seed), 15)
    return {
        "features": bell_draw(splits[0], (H, W, C), 1.0, 6.0, ((0, 4), (1, 64))),
        "depth_weight": bell_draw(splits[1], (7, 7, C), 49 ** -0.5, 0.875, (), jnp.float32),
        "depth_bias": bell_draw(splits[2], (C,), 0.5, 3.0, (), jnp.float32),
        "norm_gain": jnp.clip(1.0 + 0.18 * jax.random.normal(splits[3], (C,), jnp.float32), 0.1, 1.9),
        "norm_shift": bell_draw(splits[4], (C,), 0.3, 2.0, (), jnp.float32),
        "expand_weight": bell_draw(splits[5], (C, HID), C ** -0.5, 0.3125),
        "expand_bias": bell_draw(splits[6], (HID,), 0.5, 3.0, (), jnp.float32),
        "reduce_weight": bell_draw(splits[7], (HID, C), HID ** -0.5, 0.15625),
        "reduce_bias": bell_draw(splits[8], (C,), 0.5, 3.0, (), jnp.float32),
        "layer_scale": jnp.clip(jnp.exp(jax.random.uniform(splits[9], (C,), jnp.float32, math.log(0.3), math.log(1.5))), 0.3, 1.5),
        "down_gain": jnp.clip(1.0 + 0.18 * jax.random.normal(splits[10], (C,), jnp.float32), 0.1, 1.9),
        "down_shift": bell_draw(splits[11], (C,), 0.3, 2.0, (), jnp.float32),
        "down_weight": bell_draw(splits[12], (2, 2, C, C2), (4 * C) ** -0.5, 0.15625),
        "down_bias": bell_draw(splits[13], (C2,), 0.5, 3.0, (), jnp.float32),
    }


def layer_norm(values, gain, shift):
    center = lax.optimization_barrier(jnp.mean(values, axis=-1, keepdims=True))
    spread = lax.optimization_barrier(jnp.mean((values - center) ** 2, axis=-1, keepdims=True))
    return (values - center) * lax.rsqrt(spread + 1e-06) * gain + shift

def reference(features, depth_weight, depth_bias, norm_gain, norm_shift, expand_weight, expand_bias, reduce_weight, reduce_bias, layer_scale, down_gain, down_shift, down_weight, down_bias):
    padded = jnp.pad(features, ((3, 3), (3, 3), (0, 0)))

    def one_row(row_index):
        window = lax.dynamic_slice_in_dim(padded, row_index, 7, 0).astype(jnp.float32)
        total = jnp.broadcast_to(depth_bias.astype(jnp.float32), (W, C))
        for offset_a in range(7):
            for offset_b in range(7):
                total = total + window[offset_a, offset_b:offset_b + W] * depth_weight[offset_a, offset_b].astype(jnp.float32)
        normed = layer_norm(total, norm_gain, norm_shift).astype(jnp.bfloat16)
        hidden = jax.nn.gelu(jnp.dot(normed, expand_weight, preferred_element_type=jnp.float32) + expand_bias, approximate=False).astype(jnp.bfloat16)
        branch = jnp.dot(hidden, reduce_weight, preferred_element_type=jnp.float32) + reduce_bias
        source = lax.dynamic_index_in_dim(features, row_index, 0, keepdims=False).astype(jnp.float32)
        return (source + layer_scale * branch).astype(jnp.bfloat16)
    block_out = lax.map(one_row, jnp.arange(H, dtype=jnp.int32))
    flat_weight = down_weight.reshape(4 * C, C2)

    def one_pair(pair_index):
        pair = lax.dynamic_slice_in_dim(block_out, pair_index * 2, 2, 0).astype(jnp.float32)
        normed = layer_norm(pair, down_gain, down_shift).astype(jnp.bfloat16)
        patches = normed.reshape(2, W2, 2, C).transpose(1, 0, 2, 3).reshape(W2, 4 * C)
        return (jnp.dot(patches, flat_weight, preferred_element_type=jnp.float32) + down_bias).astype(jnp.bfloat16)
    return lax.map(one_pair, jnp.arange(H2, dtype=jnp.int32))
```

```python
import jax
import jax.numpy as jnp
from jax import lax
from jax.experimental import pallas as pl
from jax.experimental.pallas import tpu as pltpu
from jax.sharding import PartitionSpec as P

MESH = pl.DeviceIdType.MESH
F32 = jnp.float32
BF16 = jnp.bfloat16

ROWS, COLS, C, HID, C2 = 32, 128, 384, 1536, 768
LT = C // 128
PITCH = 144
LEFT = 8
STEP = 4
STEPS = ROWS // STEP
HALF = COLS // 2
M = STEP * COLS
CHUNKS = 6
HC = HID // CHUNKS


def block_kernel(
    feat, dw, db, gain, shift, w1, b1, w2, b2, scale, dgain, dshift, wd, bd,
    out,
    xin, xp, wb, cs, nb, acc, dn, sbuf, cbuf, rowh, colh, corner,
    in_sem, row_s, row_r, col_s, col_r, cor_s, cor_r, out_s, out_r, own_sem,
):
    r = lax.axis_index("rows")
    c = lax.axis_index("cols")
    nr, nc = 4, lax.axis_size("cols")
    up, down = lax.rem(r + nr - 1, nr), lax.rem(r + 1, nr)
    left, right = lax.rem(c + nc - 1, nc), lax.rem(c + 1, nc)

    load = pltpu.make_async_copy(feat, xin, in_sem)
    load.start()

    barrier = pltpu.get_barrier_semaphore()
    partners = [(lax.rem(r + j, nr), c) for j in (1, 2, 3)]
    partners += [(r, left), (r, right)]
    partners += [(up, left), (up, right), (down, left), (down, right)]
    for who in partners:
        pl.semaphore_signal(barrier, inc=1, device_id=who, device_id_type=MESH)

    for a in range(7):
        for b in range(7):
            for t in range(LT):
                wb[t, a * 7 + b] = jnp.broadcast_to(
                    dw[a, pl.ds(b, 1), pl.ds(t * 128, 128)], (8, 128)
                )

    pl.semaphore_wait(barrier, len(partners))

    def row_copy(k):
        return pltpu.make_async_remote_copy(
            src_ref=feat.at[pl.ds(0 if k == 0 else ROWS - 3, 3)],
            dst_ref=rowh.at[1 - k],
            send_sem=row_s.at[k],
            recv_sem=row_r.at[1 - k],
            device_id=(up if k == 0 else down, c),
            device_id_type=MESH,
        )

    @pl.when(r > 0)
    def _():
        row_copy(0).start()

    @pl.when(r < nr - 1)
    def _():
        row_copy(1).start()

    load.wait()

    def fill(i, carry):
        at = pl.multiple_of((i + 3) * PITCH + LEFT, 8)
        for t in range(LT):
            xp[t, pl.ds(at, COLS), :] = xin[i, :, pl.ds(t * 128, 128)].astype(F32)
        return carry

    lax.fori_loop(0, ROWS, fill, 0)

    for side in range(2):
        for j in range(3):
            at = 3 * PITCH + LEFT + (j if side == 0 else COLS - 3 + j)
            for t in range(LT):
                cbuf[side, j, :, pl.ds(t * 128, 128)] = xp[
                    t, pl.ds(at, ROWS, stride=PITCH), :
                ].astype(BF16)

    def col_copy(side):
        return pltpu.make_async_remote_copy(
            src_ref=cbuf.at[side],
            dst_ref=colh.at[1 - side],
            send_sem=col_s.at[side],
            recv_sem=col_r.at[1 - side],
            device_id=(r, left if side == 0 else right),
            device_id_type=MESH,
        )

    def corner_copy(v, side):
        return pltpu.make_async_remote_copy(
            src_ref=cbuf.at[side, :, pl.ds(16 * v, 16)],
            dst_ref=corner.at[1 - v, 1 - side],
            send_sem=cor_s.at[v, side],
            recv_sem=cor_r.at[1 - v, 1 - side],
            device_id=(up if v == 0 else down, left if side == 0 else right),
            device_id_type=MESH,
        )

    for side in range(2):
        col_copy(side).start()
    for v in range(2):
        for side in range(2):
            corner_copy(v, side).start()

    has = [(c > 0).astype(F32), (c < nc - 1).astype(F32)]
    for side in range(2):
        col_copy(1 - side).wait_recv()
        for j in range(3):
            at = 3 * PITCH + (LEFT - 3 + j if side == 0 else LEFT + COLS + j)
            for t in range(LT):
                xp[t, pl.ds(at, ROWS, stride=PITCH), :] = (
                    colh[side, j, :, pl.ds(t * 128, 128)].astype(F32) * has[side]
                )

    def fill_rows():
        for v in range(2):
            base = 0 if v == 0 else ROWS + 3
            inside = r > 0 if v == 0 else r < nr - 1
            for side in range(2):
                corner_copy(1 - v, 1 - side).wait_recv()

            @pl.when(inside)
            def _():
                row_copy(1 - v).wait_recv()
                for i in range(3):
                    for t in range(LT):
                        xp[t, pl.ds((base + i) * PITCH + LEFT, COLS), :] = rowh[
                            v, i, :, pl.ds(t * 128, 128)
                        ].astype(F32)
                for side in range(2):
                    for j in range(3):
                        at = base * PITCH + (LEFT - 3 + j if side == 0 else LEFT + COLS + j)
                        for t in range(LT):
                            piece = (
                                corner[v, side, j, :, pl.ds(t * 128, 128)].astype(F32) * has[side]
                            )
                            for i in range(3):
                                row = (13 if v == 0 else 0) + i
                                xp[t, pl.ds(at + i * PITCH, 1), :] = piece[row : row + 1]

            @pl.when(jnp.logical_not(inside))
            def _():
                for i in range(3):
                    for t in range(LT):
                        xp[t, pl.ds((base + i) * PITCH, PITCH), :] = jnp.zeros((PITCH, 128), F32)

    def conv_part(n, s):
        t = n // 2
        for q in range(4):
            jb = lax.rem(n, 2) * 4 + q
            total = [[None] * STEP, [None] * STEP]
            for o in range(8):
                x = [
                    xp[t, pl.ds((s * STEP + i) * PITCH + jb * 16 + (LEFT - 3 + o), 8, stride=2), :]
                    for i in range(STEP + 6)
                ]
                for par in range(2):
                    b = o - par
                    if 0 <= b <= 6:
                        for a in range(7):
                            w = wb[t, a * 7 + b]
                            for i in range(STEP):
                                p = x[i + a] * w
                                total[par][i] = p if total[par][i] is None else total[par][i] + p
            for par in range(2):
                for i in range(STEP):
                    at = pl.multiple_of((i * 2 + par) * HALF + jb * 8, 8)
                    cs[t, pl.ds(at, 8), :] = total[par][i]

    def mlp_part(n):
        z = jnp.dot(nb[...], w1[:, pl.ds(pl.multiple_of(n * HC, HC), HC)], preferred_element_type=F32)
        z = z + b1[:, pl.ds(pl.multiple_of(n * HC, HC), HC)]
        h = (z + z * lax.erf(z * 0.7071067811865476)).astype(BF16)
        acc[...] += jnp.dot(h, w2[pl.ds(pl.multiple_of(n * HC, HC), HC), :], preferred_element_type=F32)

    def norm(x):
        center = jnp.sum(x[0] + x[1] + x[2], axis=-1, keepdims=True) * (1.0 / C)
        x = [v - center for v in x]
        spread = jnp.sum(x[0] * x[0] + x[1] * x[1] + x[2] * x[2], axis=-1, keepdims=True) * (1.0 / C)
        f = lax.rsqrt(spread + 1e-06)
        return [v * f for v in x]

    def norm_part():
        def one(m, carry):
            at = pl.ds(pl.multiple_of(m * 64, 64), 64)
            y = norm([cs[t, at, :] + db[:, pl.ds(t * 128, 128)] for t in range(LT)])
            for t in range(LT):
                lanes = pl.ds(t * 128, 128)
                nb[at, lanes] = (y[t] * gain[:, lanes] + shift[:, lanes]).astype(BF16)
                acc[at, lanes] = jnp.zeros((64, 128), F32)
            return carry

        lax.fori_loop(0, M // 64, one, 0)

    def down_part(k, s):
        def one(m, carry):
            i, par = m // 2, lax.rem(m, 2)
            at = pl.ds(pl.multiple_of(m * 64, 64), 64)
            x = []
            for t in range(LT):
                lanes = pl.ds(t * 128, 128)
                f = xp[t, pl.ds((s * STEP + i + 3) * PITCH + LEFT + par, HALF, stride=2), :]
                v = f + scale[:, lanes] * (0.5 * acc[at, lanes] + b2[:, lanes])
                x.append(v.astype(BF16).astype(F32))
            y = norm(x)
            for t in range(LT):
                lanes = pl.ds(t * 128, 128)
                dn[m, :, lanes] = (y[t] * dgain[:, lanes] + dshift[:, lanes]).astype(BF16)
            return carry

        lax.fori_loop(0, 2 * STEP, one, 0)
        low = lax.broadcasted_iota(jnp.int32, (HALF, 128), 1) < 64
        patches = jnp.concatenate(
            [jnp.concatenate([dn[4 * p + e] for e in range(4)], axis=1) for p in range(2)], axis=0
        )
        res = jnp.dot(patches, wd[...], preferred_element_type=F32) + bd[...]
        for d in range(4):
            tile = (0, 2, 3, 5)[d] * 128
            for p in range(2):
                sbuf[d, k, p] = res[p * HALF : (p + 1) * HALF, tile : tile + 128].astype(BF16)
        for g in range(2):
            tile = (1, 4)[g] * 128
            e0, e1 = res[:HALF, tile : tile + 128], res[HALF:, tile : tile + 128]
            sbuf[2 * g, k, 2] = jnp.where(low, e0, pltpu.roll(e1, 64, 1)).astype(BF16)
            sbuf[2 * g + 1, k, 2] = jnp.where(low, pltpu.roll(e0, 64, 1), e1).astype(BF16)
        for d in range(4):
            @pl.when(r != d)
            def _():
                out_copy(d, k, s).start()

            @pl.when(r == d)
            def _():
                own_copy(d, k, s).start()

    def out_copy(d, k, s):
        return pltpu.make_async_remote_copy(
            src_ref=sbuf.at[d, k],
            dst_ref=out.at[r, s],
            send_sem=out_s.at[d, k],
            recv_sem=out_r.at[r, k],
            device_id=(d, c),
            device_id_type=MESH,
        )

    def in_copy(src, k, s):
        return pltpu.make_async_remote_copy(
            src_ref=sbuf.at[src, k],
            dst_ref=out.at[src, s],
            send_sem=out_s.at[src, k],
            recv_sem=out_r.at[src, k],
            device_id=(src, c),
            device_id_type=MESH,
        )

    def own_copy(d, k, s):
        return pltpu.make_async_copy(sbuf.at[d, k], out.at[d, s], own_sem.at[k])

    def rows_of(k):
        return lax.rem(k + 1, STEPS)

    def conv_only(n, carry):
        conv_part(n, rows_of(0))
        return carry

    lax.fori_loop(0, CHUNKS, conv_only, 0)
    norm_part()

    def step(k, carry):
        @pl.when(k == STEPS - 2)
        def _():
            fill_rows()

        s = rows_of(k)

        def both(n, carry2):
            conv_part(n, s)
            mlp_part(n)
            return carry2

        lax.fori_loop(0, CHUNKS, both, 0)
        down_part(k - 1, rows_of(k - 1))
        norm_part()
        return carry

    lax.fori_loop(1, STEPS, step, 0)

    def mlp_only(n, carry):
        mlp_part(n)
        return carry

    lax.fori_loop(0, CHUNKS, mlp_only, 0)
    down_part(STEPS - 1, rows_of(STEPS - 1))

    @pl.when(r > 0)
    def _():
        row_copy(0).wait_send()

    @pl.when(r < nr - 1)
    def _():
        row_copy(1).wait_send()

    for side in range(2):
        col_copy(side).wait_send()
        for v in range(2):
            corner_copy(v, side).wait_send()

    def finish(k, carry):
        s = rows_of(k)
        for d in range(4):
            @pl.when(r != d)
            def _():
                in_copy(d, k, s).wait_recv()
                out_copy(d, k, s).wait_send()

            @pl.when(r == d)
            def _():
                own_copy(d, k, s).wait()

        return carry

    lax.fori_loop(0, STEPS, finish, 0)


def unpack_kernel(packed, out):
    odd = lax.rem(lax.axis_index("rows"), 2)

    @pl.when(odd == 0)
    def _():
        for s in range(STEPS):
            for p in range(2):
                tail = packed[0, s, 2][:, p * 64 : (p + 1) * 64]
                out[2 * s + p] = jnp.concatenate([packed[0, s, p], tail], axis=1)

    @pl.when(odd == 1)
    def _():
        for s in range(STEPS):
            for p in range(2):
                head = packed[0, s, 2][:, p * 64 : (p + 1) * 64]
                out[2 * s + p] = jnp.concatenate([head, packed[0, s, p]], axis=1)


def per_device(
    features, depth_weight, depth_bias, norm_gain, norm_shift, expand_weight, expand_bias,
    reduce_weight, reduce_bias, layer_scale, down_gain, down_shift, down_weight, down_bias,
):
    row = lambda v: v.reshape(1, -1)
    vmem = pl.BlockSpec(memory_space=pltpu.VMEM)
    anywhere = pl.BlockSpec(memory_space=pl.ANY)
    dma = pltpu.SemaphoreType.DMA
    packed = pl.pallas_call(
        block_kernel,
        out_shape=jax.ShapeDtypeStruct((4, STEPS, 3, HALF, 128), BF16),
        in_specs=[anywhere] + [vmem] * 13,
        out_specs=anywhere,
        scratch_shapes=[
            pltpu.VMEM((ROWS, COLS, C), BF16),
            pltpu.VMEM((LT, (ROWS + 6) * PITCH, 128), F32),
            pltpu.VMEM((LT, 49, 8, 128), F32),
            pltpu.VMEM((LT, M, 128), F32),
            pltpu.VMEM((M, C), BF16),
            pltpu.VMEM((M, C), F32),
            pltpu.VMEM((2 * STEP, HALF, C), BF16),
            pltpu.VMEM((4, STEPS, 3, HALF, 128), BF16),
            pltpu.VMEM((2, 3, ROWS, C), BF16),
            pltpu.VMEM((2, 3, COLS, C), BF16),
            pltpu.VMEM((2, 3, ROWS, C), BF16),
            pltpu.VMEM((2, 2, 3, 16, C), BF16),
            dma, dma((2,)), dma((2,)), dma((2,)), dma((2,)), dma((2, 2)), dma((2, 2)),
            dma((4, STEPS)), dma((4, STEPS)), dma((STEPS,)),
        ],
        compiler_params=pltpu.CompilerParams(
            collective_id=0, has_side_effects=True, vmem_limit_bytes=56 * 2**20
        ),
    )(
        features, depth_weight, row(depth_bias), row(norm_gain), row(norm_shift), expand_weight,
        row(expand_bias), reduce_weight, row(reduce_bias), row(layer_scale), row(down_gain),
        row(down_shift), down_weight.reshape(4 * C, C2), row(down_bias),
    )
    return pl.pallas_call(
        unpack_kernel,
        grid=(4,),
        out_shape=jax.ShapeDtypeStruct((64, HALF, C2 // 4), BF16),
        in_specs=[pl.BlockSpec((1, STEPS, 3, HALF, 128), lambda i: (i, 0, 0, 0, 0))],
        out_specs=pl.BlockSpec((16, HALF, C2 // 4), lambda i: (i, 0, 0)),
    )(packed)


def solution(mesh):
    in_specs = (P("rows", "cols", None),) + (P(),) * 13
    return jax.shard_map(
        per_device, mesh=mesh, in_specs=in_specs, out_specs=P(None, "cols", "rows"), check_vma=False
    )
```

```python
import jax
import jax.numpy as jnp
from jax import lax
from jax.experimental import pallas as pl
from jax.experimental.pallas import tpu as pltpu
from jax.sharding import PartitionSpec as P

MESH = pl.DeviceIdType.MESH
F32 = jnp.float32
BF16 = jnp.bfloat16

ROWS, COLS, C, HID, C2 = 32, 128, 384, 1536, 768
LT = C // 128
PITCH = 144
LEFT = 8
STEP = 4
STEPS = ROWS // STEP
HALF = COLS // 2
M = STEP * COLS
CHUNKS = 6
HC = HID // CHUNKS


def block_kernel(
    feat, dw_hbm, db, gain, shift, w1_hbm, b1_hbm, w2_hbm, b2, scale, dgain, dshift, wd_hbm, bd_hbm,
    out,
    xin, xp, dw, v0, v1, v2, v3, v4, v5, v6, b1_in, bd_in, wb, pv, b1, bd, w1, w2, wd, nb_new, nb, acc, acc_done, patches, sbuf,
    cbuf, rowh, colh, corner,
    in_sem, w_sem, p_sem, row_s, row_r, col_s, col_r, cor_s, cor_r, out_s, out_r, own_sem,
):
    r = lax.axis_index("rows")
    c = lax.axis_index("cols")
    nr, nc = 4, lax.axis_size("cols")
    up, down = lax.rem(r + nr - 1, nr), lax.rem(r + 1, nr)
    left, right = lax.rem(c + nc - 1, nc), lax.rem(c + 1, nc)

    barrier = pltpu.get_barrier_semaphore()
    partners = [(lax.rem(r + j, nr), c) for j in (1, 2, 3)]
    partners += [(r, left), (r, right)]
    partners += [(up, left), (up, right), (down, left), (down, right)]
    for who in partners:
        pl.semaphore_signal(barrier, inc=1, device_id=who, device_id_type=MESH)

    spans = [(0, 16), (COLS - 16, 16), (16, COLS - 32)]
    loads = [
        pltpu.make_async_copy(
            feat.at[:, pl.ds(at, size)], xin.at[:, pl.ds(at, size)], in_sem.at[n]
        )
        for n, (at, size) in enumerate(spans)
    ]
    loads += [
        pltpu.make_async_copy(src, dst, w_sem.at[n])
        for n, (src, dst) in enumerate([(w1_hbm, w1), (w2_hbm, w2), (wd_hbm, wd)])
    ]
    vecs = (v0, v1, v2, v3, v4, v5, v6)
    small = list(zip((db, gain, shift, b2, scale, dgain, dshift), vecs))
    small += [(dw_hbm, dw), (b1_hbm, b1_in), (bd_hbm, bd_in)]
    small = [pltpu.make_async_copy(src, dst, p_sem.at[n]) for n, (src, dst) in enumerate(small)]
    for load in loads[:2] + small + loads[2:]:
        load.start()

    def vec(n, t):
        return pv[pl.ds(n, 1), pl.ds(t * 128, 128)]

    def fill(span):
        at, size = span

        def one(i, carry):
            to = pl.multiple_of((i + 3) * PITCH + LEFT + at, 8)
            for t in range(LT):
                xp[t, pl.ds(to, size), :] = xin[i, pl.ds(at, size), pl.ds(t * 128, 128)].astype(F32)
            return carry

        lax.fori_loop(0, ROWS, one, 0, unroll=4)

    for side in range(2):
        loads[side].wait()
        fill(spans[side])
        for j in range(3):
            at = 3 * PITCH + LEFT + (j if side == 0 else COLS - 3 + j)
            for t in range(LT):
                cbuf[side, j, :, pl.ds(t * 128, 128)] = xp[
                    t, pl.ds(at, ROWS, stride=PITCH), :
                ].astype(BF16)

    pl.semaphore_wait(barrier, len(partners))

    def col_copy(side):
        return pltpu.make_async_remote_copy(
            src_ref=cbuf.at[side],
            dst_ref=colh.at[1 - side],
            send_sem=col_s.at[side],
            recv_sem=col_r.at[1 - side],
            device_id=(r, left if side == 0 else right),
            device_id_type=MESH,
        )

    def corner_copy(v, side):
        return pltpu.make_async_remote_copy(
            src_ref=cbuf.at[side, :, pl.ds(16 * v, 16)],
            dst_ref=corner.at[1 - v, 1 - side],
            send_sem=cor_s.at[v, side],
            recv_sem=cor_r.at[1 - v, 1 - side],
            device_id=(up if v == 0 else down, left if side == 0 else right),
            device_id_type=MESH,
        )

    def row_copy(k):
        return pltpu.make_async_remote_copy(
            src_ref=feat.at[pl.ds(0 if k == 0 else ROWS - 3, 3)],
            dst_ref=rowh.at[1 - k],
            send_sem=row_s.at[k],
            recv_sem=row_r.at[1 - k],
            device_id=(up if k == 0 else down, c),
            device_id_type=MESH,
        )

    for side in range(2):
        col_copy(side).start()
    for v in range(2):
        for side in range(2):
            corner_copy(v, side).start()

    @pl.when(r > 0)
    def _():
        row_copy(0).start()

    @pl.when(r < nr - 1)
    def _():
        row_copy(1).start()

    for load in small:
        load.wait()
    for a in range(7):
        for b in range(7):
            for t in range(LT):
                wb[t, a * 7 + b] = jnp.broadcast_to(
                    dw[a, pl.ds(b, 1), pl.ds(t * 128, 128)], (8, 128)
                )
    for n in range(7):
        pv[pl.ds(n, 1), :] = vecs[n][...].reshape(1, C)
    b1[...] = b1_in[...].reshape(1, HID)
    bd[...] = bd_in[...].reshape(1, C2)

    loads[2].wait()
    fill(spans[2])

    has = [(c > 0).astype(F32), (c < nc - 1).astype(F32)]

    def fill_cols():
        for side in range(2):
            col_copy(1 - side).wait_recv()
            for j in range(3):
                at = 3 * PITCH + (LEFT - 3 + j if side == 0 else LEFT + COLS + j)
                for t in range(LT):
                    xp[t, pl.ds(at, ROWS, stride=PITCH), :] = (
                        colh[side, j, :, pl.ds(t * 128, 128)].astype(F32) * has[side]
                    )

    def fill_rows():
        for v in range(2):
            base = 0 if v == 0 else ROWS + 3
            inside = r > 0 if v == 0 else r < nr - 1
            for side in range(2):
                corner_copy(1 - v, 1 - side).wait_recv()

            @pl.when(inside)
            def _():
                row_copy(1 - v).wait_recv()
                for i in range(3):
                    for t in range(LT):
                        xp[t, pl.ds((base + i) * PITCH + LEFT, COLS), :] = rowh[
                            v, i, :, pl.ds(t * 128, 128)
                        ].astype(F32)
                for side in range(2):
                    for j in range(3):
                        at = base * PITCH + (LEFT - 3 + j if side == 0 else LEFT + COLS + j)
                        for t in range(LT):
                            piece = (
                                corner[v, side, j, :, pl.ds(t * 128, 128)].astype(F32) * has[side]
                            )
                            for i in range(3):
                                row = (13 if v == 0 else 0) + i
                                xp[t, pl.ds(at + i * PITCH, 1), :] = piece[row : row + 1]

            @pl.when(jnp.logical_not(inside))
            def _():
                for i in range(3):
                    for t in range(LT):
                        xp[t, pl.ds((base + i) * PITCH, PITCH), :] = jnp.zeros((PITCH, 128), F32)

    def norm(x):
        center = jnp.sum(x[0] + x[1] + x[2], axis=-1, keepdims=True) * (1.0 / C)
        x = [v - center for v in x]
        spread = jnp.sum(x[0] * x[0] + x[1] * x[1] + x[2] * x[2], axis=-1, keepdims=True) * (1.0 / C)
        f = lax.rsqrt(spread + 1e-06)
        return [v * f for v in x]

    def conv_part(jb, s):
        whole = []
        for t in range(LT):
            total = [[None] * 2 for _ in range(STEP)]
            for o in range(8):
                x = [
                    xp[t, pl.ds((s * STEP + i) * PITCH + jb * 16 + (LEFT - 3 + o), 8, stride=2), :]
                    for i in range(STEP + 6)
                ]
                for par in range(2):
                    b = o - par
                    if 0 <= b <= 6:
                        for a in range(7):
                            w = wb[t, a * 7 + b]
                            for i in range(STEP):
                                p = x[i + a] * w
                                before = total[i][par]
                                total[i][par] = p if before is None else before + p
            whole.append(
                jnp.concatenate([total[i][par] for i in range(STEP) for par in range(2)], axis=0)
                + vec(0, t)
            )
        y = norm(whole)
        at = pl.ds(pl.multiple_of(jb * 64, 64), 64)
        for t in range(LT):
            nb_new[at, pl.ds(t * 128, 128)] = (y[t] * vec(1, t) + vec(2, t)).astype(BF16)

    def mlp_part(n):
        at = pl.ds(pl.multiple_of(n * HC, HC), HC)
        z = jnp.dot(nb[...], w1[:, at], preferred_element_type=F32) + b1[:, at]
        h = (z + z * lax.erf(z * 0.7071067811865476)).astype(BF16)
        acc[...] += jnp.dot(h, w2[at, :], preferred_element_type=F32)

    def turn():
        nb[...] = nb_new[...]
        acc_done[...] = acc[...]
        acc[...] = jnp.zeros_like(acc)

    def norm_part(jb, s):
        at = pl.ds(pl.multiple_of(jb * 64, 64), 64)
        x = []
        for t in range(LT):
            f = jnp.concatenate(
                [
                    xp[t, pl.ds((s * STEP + i + 3) * PITCH + jb * 16 + (LEFT + par), 8, stride=2), :]
                    for i in range(STEP)
                    for par in range(2)
                ],
                axis=0,
            )
            v = f + vec(4, t) * (0.5 * acc_done[at, pl.ds(t * 128, 128)] + vec(3, t))
            x.append(v.astype(BF16).astype(F32))
        y = norm(x)
        for t in range(LT):
            v = y[t] * vec(5, t) + vec(6, t)
            for a in range(2):
                for par in range(2):
                    e = a * 2 + par
                    both = jnp.concatenate([v[e * 8 : e * 8 + 8], v[e * 8 + 32 : e * 8 + 40]], axis=0)
                    patches[
                        pl.ds(pl.multiple_of(jb * 16, 16), 16), pl.ds(e * C + t * 128, 128)
                    ] = both.astype(BF16)

    def down_part(k, s):
        low = lax.broadcasted_iota(jnp.int32, (HALF, 128), 1) < 64
        res = jnp.dot(patches[...], wd[...], preferred_element_type=F32) + bd[...]

        def piece(p, tile):
            return jnp.concatenate(
                [res[q * 16 + p * 8 : q * 16 + p * 8 + 8, tile * 128 : tile * 128 + 128] for q in range(8)],
                axis=0,
            )

        for d in range(4):
            for p in range(2):
                sbuf[d, k, p] = piece(p, (0, 2, 3, 5)[d]).astype(BF16)
        for g in range(2):
            e0, e1 = piece(0, (1, 4)[g]), piece(1, (1, 4)[g])
            sbuf[2 * g, k, 2] = jnp.where(low, e0, pltpu.roll(e1, 64, 1)).astype(BF16)
            sbuf[2 * g + 1, k, 2] = jnp.where(low, pltpu.roll(e0, 64, 1), e1).astype(BF16)
        for d in range(4):
            @pl.when(r != d)
            def _():
                out_copy(d, k, s).start()

            @pl.when(r == d)
            def _():
                own_copy(d, k, s).start()

    def out_copy(d, k, s):
        return pltpu.make_async_remote_copy(
            src_ref=sbuf.at[d, k],
            dst_ref=out.at[r, s],
            send_sem=out_s.at[d, k],
            recv_sem=out_r.at[r, k],
            device_id=(d, c),
            device_id_type=MESH,
        )

    def in_copy(src, k, s):
        return pltpu.make_async_remote_copy(
            src_ref=sbuf.at[src, k],
            dst_ref=out.at[src, s],
            send_sem=out_s.at[src, k],
            recv_sem=out_r.at[src, k],
            device_id=(src, c),
            device_id_type=MESH,
        )

    def own_copy(d, k, s):
        return pltpu.make_async_copy(sbuf.at[d, k], out.at[d, s], own_sem.at[k])

    def rows_of(k):
        return lax.rem(k + 1, STEPS)

    def first(q, carry):
        @pl.when(q == 6)
        def _():
            fill_cols()

        conv_part(jnp.where(q == 6, 0, jnp.where(q == 7, 7, q + 1)), rows_of(0))
        return carry

    lax.fori_loop(0, 8, first, 0)
    for load in loads[3:]:
        load.wait()
    acc[...] = jnp.zeros_like(acc)
    acc_done[...] = jnp.zeros_like(acc)
    nb[...] = nb_new[...]

    def step(k, carry):
        @pl.when(k == STEPS - 2)
        def _():
            fill_rows()

        s = rows_of(k)
        s_old = rows_of(k + STEPS - 2)

        def part(h, carry2):
            for q in range(4):
                conv_part(h * 4 + q, s)
                if q < 3:
                    mlp_part(h * 3 + q)
                norm_part(h * 4 + q, s_old)
            return carry2

        lax.fori_loop(0, 2, part, 0)

        @pl.when(k >= 2)
        def _():
            down_part(k - 2, s_old)

        turn()
        return carry

    lax.fori_loop(1, STEPS, step, 0)

    def late(h, carry):
        for q in range(4):
            if q < 3:
                mlp_part(h * 3 + q)
            norm_part(h * 4 + q, rows_of(STEPS - 2))
        return carry

    lax.fori_loop(0, 2, late, 0)
    down_part(STEPS - 2, rows_of(STEPS - 2))
    turn()

    def last(h, carry):
        for q in range(4):
            norm_part(h * 4 + q, rows_of(STEPS - 1))
        return carry

    lax.fori_loop(0, 2, last, 0)
    down_part(STEPS - 1, rows_of(STEPS - 1))

    @pl.when(r > 0)
    def _():
        row_copy(0).wait_send()

    @pl.when(r < nr - 1)
    def _():
        row_copy(1).wait_send()

    for side in range(2):
        col_copy(side).wait_send()
        for v in range(2):
            corner_copy(v, side).wait_send()

    def finish(k, carry):
        s = rows_of(k)
        for d in range(4):
            @pl.when(r != d)
            def _():
                in_copy(d, k, s).wait_recv()
                out_copy(d, k, s).wait_send()

            @pl.when(r == d)
            def _():
                own_copy(d, k, s).wait()

        return carry

    lax.fori_loop(0, STEPS, finish, 0)


def unpack_kernel(packed, out):
    odd = lax.rem(lax.axis_index("rows"), 2)

    @pl.when(odd == 0)
    def _():
        for s in range(STEPS):
            for p in range(2):
                tail = packed[0, s, 2][:, p * 64 : (p + 1) * 64]
                out[2 * s + p] = jnp.concatenate([packed[0, s, p], tail], axis=1)

    @pl.when(odd == 1)
    def _():
        for s in range(STEPS):
            for p in range(2):
                head = packed[0, s, 2][:, p * 64 : (p + 1) * 64]
                out[2 * s + p] = jnp.concatenate([head, packed[0, s, p]], axis=1)


def per_device(
    features, depth_weight, depth_bias, norm_gain, norm_shift, expand_weight, expand_bias,
    reduce_weight, reduce_bias, layer_scale, down_gain, down_shift, down_weight, down_bias,
):
    anywhere = pl.BlockSpec(memory_space=pl.ANY)
    dma = pltpu.SemaphoreType.DMA
    packed = pl.pallas_call(
        block_kernel,
        out_shape=jax.ShapeDtypeStruct((4, STEPS, 3, HALF, 128), BF16),
        in_specs=[anywhere] * 14,
        out_specs=anywhere,
        scratch_shapes=[
            pltpu.VMEM((ROWS, COLS, C), BF16),
            pltpu.VMEM((LT, (ROWS + 6) * PITCH, 128), F32),
            pltpu.VMEM((7, 7, C), F32),
            *[pltpu.VMEM((C,), F32) for _ in range(7)],
            pltpu.VMEM((HID,), F32),
            pltpu.VMEM((C2,), F32),
            pltpu.VMEM((LT, 49, 8, 128), F32),
            pltpu.VMEM((8, C), F32),
            pltpu.VMEM((1, HID), F32),
            pltpu.VMEM((1, C2), F32),
            pltpu.VMEM((C, HID), BF16),
            pltpu.VMEM((HID, C), BF16),
            pltpu.VMEM((4 * C, C2), BF16),
            pltpu.VMEM((M, C), BF16),
            pltpu.VMEM((M, C), BF16),
            pltpu.VMEM((M, C), F32),
            pltpu.VMEM((M, C), F32),
            pltpu.VMEM((2 * HALF, 4 * C), BF16),
            pltpu.VMEM((4, STEPS, 3, HALF, 128), BF16),
            pltpu.VMEM((2, 3, ROWS, C), BF16),
            pltpu.VMEM((2, 3, COLS, C), BF16),
            pltpu.VMEM((2, 3, ROWS, C), BF16),
            pltpu.VMEM((2, 2, 3, 16, C), BF16),
            dma((3,)), dma((3,)), dma((10,)), dma((2,)), dma((2,)), dma((2,)), dma((2,)), dma((2, 2)), dma((2, 2)),
            dma((4, STEPS)), dma((4, STEPS)), dma((STEPS,)),
        ],
        compiler_params=pltpu.CompilerParams(
            collective_id=0, has_side_effects=True, vmem_limit_bytes=56 * 2**20
        ),
    )(
        features, depth_weight, depth_bias, norm_gain, norm_shift, expand_weight, expand_bias,
        reduce_weight, reduce_bias, layer_scale, down_gain, down_shift,
        down_weight.reshape(4 * C, C2), down_bias,
    )
    return pl.pallas_call(
        unpack_kernel,
        grid=(4,),
        out_shape=jax.ShapeDtypeStruct((64, HALF, C2 // 4), BF16),
        in_specs=[pl.BlockSpec((1, STEPS, 3, HALF, 128), lambda i: (i, 0, 0, 0, 0))],
        out_specs=pl.BlockSpec((16, HALF, C2 // 4), lambda i: (i, 0, 0)),
    )(packed)


def solution(mesh):
    in_specs = (P("rows", "cols", None),) + (P(),) * 13
    return jax.shard_map(
        per_device, mesh=mesh, in_specs=in_specs, out_specs=P(None, "cols", "rows"), check_vma=False
    )
```

```python
import jax
import jax.numpy as jnp
from jax import lax
from jax.experimental import pallas as pl
from jax.experimental.pallas import tpu as pltpu
from jax.sharding import PartitionSpec as P

MESH = pl.DeviceIdType.MESH
F32 = jnp.float32
BF16 = jnp.bfloat16

ROWS, COLS, C, HID, C2 = 32, 128, 384, 1536, 768
LT = C // 128
PITCH = 144
LEFT = 8
STEP = 4
STEPS = ROWS // STEP
HALF = COLS // 2
M = STEP * COLS
CHUNKS = 6
HC = HID // CHUNKS


def block_kernel(
    feat, dw_hbm, db, gain, shift, w1_hbm, b1_hbm, w2_hbm, b2, scale, dgain, dshift, wd_hbm, bd_hbm,
    out,
    xin, xp, cs, dw, v0, v1, v2, v3, v4, v5, v6, b1_in, bd_in, wb, pv, b1, bd, w1, w2, wd, nb_next, nb_new, nb, acc, acc_done, patches, sbuf,
    cbuf, rowh, colh, corner,
    in_sem, w_sem, p_sem, row_s, row_r, col_s, col_r, cor_s, cor_r, out_s, out_r, own_sem,
):
    r = lax.axis_index("rows")
    c = lax.axis_index("cols")
    nr, nc = 4, lax.axis_size("cols")
    up, down = lax.rem(r + nr - 1, nr), lax.rem(r + 1, nr)
    left, right = lax.rem(c + nc - 1, nc), lax.rem(c + 1, nc)

    spans = [(0, 16), (COLS - 16, 16), (16, COLS - 32)]
    loads = [
        pltpu.make_async_copy(
            feat.at[:, pl.ds(at, size)], xin.at[:, pl.ds(at, size)], in_sem.at[n]
        )
        for n, (at, size) in enumerate(spans)
    ]
    loads += [
        pltpu.make_async_copy(src, dst, w_sem.at[n])
        for n, (src, dst) in enumerate([(w1_hbm, w1), (w2_hbm, w2), (wd_hbm, wd)])
    ]
    vecs = (v0, v1, v2, v3, v4, v5, v6)
    small = list(zip((db, gain, shift, b2, scale, dgain, dshift), vecs))
    small += [(dw_hbm, dw), (b1_hbm, b1_in), (bd_hbm, bd_in)]
    small = [pltpu.make_async_copy(src, dst, p_sem.at[n]) for n, (src, dst) in enumerate(small)]
    for load in loads[:2] + small + loads[2:]:
        load.start()

    barrier = pltpu.get_barrier_semaphore()
    partners = [(lax.rem(r + j, nr), c) for j in (1, 2, 3)]
    partners += [(r, left), (r, right)]
    for who in partners:
        pl.semaphore_signal(barrier, inc=1, device_id=who, device_id_type=MESH)

    def vec(n, t):
        return pv[pl.ds(n, 1), pl.ds(t * 128, 128)]

    def fill(span):
        at, size = span

        def one(i, carry):
            to = pl.multiple_of((i + 3) * PITCH + LEFT + at, 8)
            for t in range(LT):
                xp[t, pl.ds(to, size), :] = xin[i, pl.ds(at, size), pl.ds(t * 128, 128)].astype(F32)
            return carry

        lax.fori_loop(0, ROWS, one, 0, unroll=4)

    for side in range(2):
        loads[side].wait()
        fill(spans[side])
        for j in range(3):
            at = 3 * PITCH + LEFT + (j if side == 0 else COLS - 3 + j)
            for t in range(LT):
                cbuf[side, j, :, pl.ds(t * 128, 128)] = xp[
                    t, pl.ds(at, ROWS, stride=PITCH), :
                ].astype(BF16)

    def col_copy(side):
        return pltpu.make_async_remote_copy(
            src_ref=cbuf.at[side],
            dst_ref=colh.at[1 - side],
            send_sem=col_s.at[side],
            recv_sem=col_r.at[1 - side],
            device_id=(r, left if side == 0 else right),
            device_id_type=MESH,
        )

    def corner_copy(v, side):
        return pltpu.make_async_remote_copy(
            src_ref=colh.at[side, :, pl.ds(16 * v, 16)],
            dst_ref=corner.at[1 - v, side],
            send_sem=cor_s.at[v, side],
            recv_sem=cor_r.at[1 - v, side],
            device_id=(up if v == 0 else down, c),
            device_id_type=MESH,
        )

    def row_copy(k):
        return pltpu.make_async_remote_copy(
            src_ref=feat.at[pl.ds(0 if k == 0 else ROWS - 3, 3)],
            dst_ref=rowh.at[1 - k],
            send_sem=row_s.at[k],
            recv_sem=row_r.at[1 - k],
            device_id=(up if k == 0 else down, c),
            device_id_type=MESH,
        )

    def send_halo():
        pl.semaphore_wait(barrier, len(partners))
        for side in range(2):
            col_copy(side).start()

        @pl.when(r > 0)
        def _():
            row_copy(0).start()

        @pl.when(r < nr - 1)
        def _():
            row_copy(1).start()

    for load in small:
        load.wait()
    for a in range(7):
        for b in range(7):
            for t in range(LT):
                wb[t, a * 7 + b] = jnp.broadcast_to(
                    dw[a, pl.ds(b, 1), pl.ds(t * 128, 128)], (8, 128)
                )
    for n in range(7):
        pv[pl.ds(n, 1), :] = vecs[n][...].reshape(1, C)
    b1[...] = b1_in[...].reshape(1, HID)
    bd[...] = bd_in[...].reshape(1, C2)

    loads[2].wait()
    fill(spans[2])

    has = [(c > 0).astype(F32), (c < nc - 1).astype(F32)]

    def fill_cols():
        for side in range(2):
            col_copy(1 - side).wait_recv()
            for v in range(2):
                corner_copy(v, side).start()
            for j in range(3):
                at = 3 * PITCH + (LEFT - 3 + j if side == 0 else LEFT + COLS + j)
                for t in range(LT):
                    xp[t, pl.ds(at, ROWS, stride=PITCH), :] = (
                        colh[side, j, :, pl.ds(t * 128, 128)].astype(F32) * has[side]
                    )

    def fill_rows():
        for v in range(2):
            base = 0 if v == 0 else ROWS + 3
            inside = r > 0 if v == 0 else r < nr - 1
            for side in range(2):
                corner_copy(1 - v, side).wait_recv()

            @pl.when(inside)
            def _():
                row_copy(1 - v).wait_recv()
                for i in range(3):
                    for t in range(LT):
                        xp[t, pl.ds((base + i) * PITCH + LEFT, COLS), :] = rowh[
                            v, i, :, pl.ds(t * 128, 128)
                        ].astype(F32)
                for side in range(2):
                    for j in range(3):
                        at = base * PITCH + (LEFT - 3 + j if side == 0 else LEFT + COLS + j)
                        for t in range(LT):
                            piece = (
                                corner[v, side, j, :, pl.ds(t * 128, 128)].astype(F32) * has[side]
                            )
                            for i in range(3):
                                row = (13 if v == 0 else 0) + i
                                xp[t, pl.ds(at + i * PITCH, 1), :] = piece[row : row + 1]

            @pl.when(jnp.logical_not(inside))
            def _():
                for i in range(3):
                    for t in range(LT):
                        xp[t, pl.ds((base + i) * PITCH, PITCH), :] = jnp.zeros((PITCH, 128), F32)

    def norm(x):
        center = jnp.sum(x[0] + x[1] + x[2], axis=-1, keepdims=True) * (1.0 / C)
        x = [v - center for v in x]
        spread = jnp.sum(x[0] * x[0] + x[1] * x[1] + x[2] * x[2], axis=-1, keepdims=True) * (1.0 / C)
        f = lax.rsqrt(spread + 1e-06)
        return [v * f for v in x]

    def conv_block(jb, s, slot, t):
        base = s * STEP * PITCH + jb * 16 + (LEFT - 3)
        total = [[None] * 2 for _ in range(STEP)]
        for a in range(7):
            for i in range(STEP):
                x = [xp[t, pl.ds(base + (i + a) * PITCH + o, 8, stride=2), :] for o in range(8)]
                for b in range(7):
                    w = wb[t, a * 7 + b]
                    for par in range(2):
                        p = x[b + par] * w
                        before = total[i][par]
                        total[i][par] = p if before is None else before + p
        for i in range(STEP):
            for par in range(2):
                at = (i * 2 + par) * 8
                cs[slot, t, at : at + 8, :] = total[i][par]

    def conv_part(jb, s, slot):
        for t in range(LT):
            conv_block(jb, s, slot, t)

    def norm1_part(jb, slot, to):
        y = norm([cs[slot, t] + vec(0, t) for t in range(LT)])
        at = pl.ds(pl.multiple_of(jb * 64, 64), 64)
        for t in range(LT):
            to[at, pl.ds(t * 128, 128)] = (y[t] * vec(1, t) + vec(2, t)).astype(BF16)

    def mlp_part(n):
        at = pl.ds(pl.multiple_of(n * HC, HC), HC)
        z = jnp.dot(nb[...], w1[:, at], preferred_element_type=F32) + b1[:, at]
        h = (z + z * lax.erf(z * 0.7071067811865476)).astype(BF16)
        acc[...] += jnp.dot(h, w2[at, :], preferred_element_type=F32)

    def turn():
        nb[...] = nb_new[...]
        nb_new[...] = nb_next[...]
        acc_done[...] = acc[...]
        acc[...] = jnp.zeros_like(acc)

    def norm_part(jb, s):
        at = pl.ds(pl.multiple_of(jb * 64, 64), 64)
        x = []
        for t in range(LT):
            f = jnp.concatenate(
                [
                    xp[t, pl.ds((s * STEP + i + 3) * PITCH + jb * 16 + (LEFT + par), 8, stride=2), :]
                    for i in range(STEP)
                    for par in range(2)
                ],
                axis=0,
            )
            v = f + vec(4, t) * (0.5 * acc_done[at, pl.ds(t * 128, 128)] + vec(3, t))
            x.append(v.astype(BF16).astype(F32))
        y = norm(x)
        for t in range(LT):
            v = y[t] * vec(5, t) + vec(6, t)
            for a in range(2):
                for par in range(2):
                    e = a * 2 + par
                    both = jnp.concatenate([v[e * 8 : e * 8 + 8], v[e * 8 + 32 : e * 8 + 40]], axis=0)
                    patches[
                        pl.ds(pl.multiple_of(jb * 16, 16), 16), pl.ds(e * C + t * 128, 128)
                    ] = both.astype(BF16)

    def down_part(k, s):
        low = lax.broadcasted_iota(jnp.int32, (HALF, 128), 1) < 64
        res = jnp.dot(patches[...], wd[...], preferred_element_type=F32) + bd[...]

        def piece(p, tile):
            return jnp.concatenate(
                [res[q * 16 + p * 8 : q * 16 + p * 8 + 8, tile * 128 : tile * 128 + 128] for q in range(8)],
                axis=0,
            )

        for d in range(4):
            for p in range(2):
                sbuf[d, k, p] = piece(p, (0, 2, 3, 5)[d]).astype(BF16)
        for g in range(2):
            e0, e1 = piece(0, (1, 4)[g]), piece(1, (1, 4)[g])
            sbuf[2 * g, k, 2] = jnp.where(low, e0, pltpu.roll(e1, 64, 1)).astype(BF16)
            sbuf[2 * g + 1, k, 2] = jnp.where(low, pltpu.roll(e0, 64, 1), e1).astype(BF16)
        for d in range(4):
            @pl.when(r != d)
            def _():
                out_copy(d, k, s).start()

            @pl.when(r == d)
            def _():
                own_copy(d, k, s).start()

    def out_copy(d, k, s):
        return pltpu.make_async_remote_copy(
            src_ref=sbuf.at[d, k],
            dst_ref=out.at[r, s],
            send_sem=out_s.at[d, k],
            recv_sem=out_r.at[r, k],
            device_id=(d, c),
            device_id_type=MESH,
        )

    def in_copy(src, k, s):
        return pltpu.make_async_remote_copy(
            src_ref=sbuf.at[src, k],
            dst_ref=out.at[src, s],
            send_sem=out_s.at[src, k],
            recv_sem=out_r.at[src, k],
            device_id=(src, c),
            device_id_type=MESH,
        )

    def own_copy(d, k, s):
        return pltpu.make_async_copy(sbuf.at[d, k], out.at[d, s], own_sem.at[k])

    def rows_of(k):
        return lax.rem(k + 1, STEPS)

    def inner(k):
        def one(n, carry):
            jb = n // 3 + 1
            conv_block(jb, rows_of(k), 8 * k + jb, lax.rem(n, 3))
            return carry

        lax.fori_loop(0, 18, one, 0)

    def outer(k):
        def one(n, carry):
            jb = 7 * (n // 3)
            conv_block(jb, rows_of(k), 8 * k + jb, lax.rem(n, 3))
            return carry

        lax.fori_loop(0, 6, one, 0)

    inner(0)
    send_halo()
    inner(1)
    for jb in range(1, 7):
        norm1_part(jb, jb, nb)
        norm1_part(jb, 8 + jb, nb_new)
    fill_cols()
    outer(0)
    outer(1)
    for jb in (0, 7):
        norm1_part(jb, jb, nb)
        norm1_part(jb, 8 + jb, nb_new)
    for load in loads[3:]:
        load.wait()
    acc[...] = jnp.zeros_like(acc)
    acc_done[...] = jnp.zeros_like(acc)
    def step(k, carry):
        @pl.when(k == STEPS - 3)
        def _():
            fill_rows()

        s = rows_of(k + 1)
        s_old = rows_of(k + STEPS - 2)

        def part(h, carry2):
            for q in range(4):
                conv_part(h * 4 + q, s, q)
                if q < 3:
                    mlp_part(h * 3 + q)
                norm1_part(h * 4 + q, q, nb_next)
                norm_part(h * 4 + q, s_old)
            return carry2

        lax.fori_loop(0, 2, part, 0)

        @pl.when(k >= 2)
        def _():
            down_part(k - 2, s_old)

        turn()
        return carry

    lax.fori_loop(1, STEPS - 1, step, 0)

    def late(k, carry):
        s_old = rows_of(k - 2)

        def part(h, carry2):
            for q in range(4):
                if q < 3:
                    mlp_part(h * 3 + q)
                norm_part(h * 4 + q, s_old)
            return carry2

        lax.fori_loop(0, 2, part, 0)
        down_part(k - 2, s_old)
        turn()
        return carry

    lax.fori_loop(STEPS - 1, STEPS + 1, late, 0)

    def last(h, carry):
        for q in range(4):
            norm_part(h * 4 + q, rows_of(STEPS - 1))
        return carry

    lax.fori_loop(0, 2, last, 0)
    down_part(STEPS - 1, rows_of(STEPS - 1))

    @pl.when(r > 0)
    def _():
        row_copy(0).wait_send()

    @pl.when(r < nr - 1)
    def _():
        row_copy(1).wait_send()

    for side in range(2):
        col_copy(side).wait_send()
        for v in range(2):
            corner_copy(v, side).wait_send()

    def finish(k, carry):
        s = rows_of(k)
        for d in range(4):
            @pl.when(r != d)
            def _():
                in_copy(d, k, s).wait_recv()
                out_copy(d, k, s).wait_send()

            @pl.when(r == d)
            def _():
                own_copy(d, k, s).wait()

        return carry

    lax.fori_loop(0, STEPS, finish, 0)


def unpack_kernel(packed, out):
    odd = lax.rem(lax.axis_index("rows"), 2)
    parts = [(n, s, p) for n in range(2) for s in range(STEPS) for p in range(2)]

    @pl.when(odd == 0)
    def _():
        for n, s, p in parts:
            tail = packed[n, s, 2][:, p * 64 : (p + 1) * 64]
            out[16 * n + 2 * s + p] = jnp.concatenate([packed[n, s, p], tail], axis=1)

    @pl.when(odd == 1)
    def _():
        for n, s, p in parts:
            head = packed[n, s, 2][:, p * 64 : (p + 1) * 64]
            out[16 * n + 2 * s + p] = jnp.concatenate([head, packed[n, s, p]], axis=1)


def per_device(
    features, depth_weight, depth_bias, norm_gain, norm_shift, expand_weight, expand_bias,
    reduce_weight, reduce_bias, layer_scale, down_gain, down_shift, down_weight, down_bias,
):
    anywhere = pl.BlockSpec(memory_space=pl.ANY)
    dma = pltpu.SemaphoreType.DMA
    packed = pl.pallas_call(
        block_kernel,
        out_shape=jax.ShapeDtypeStruct((4, STEPS, 3, HALF, 128), BF16),
        in_specs=[anywhere] * 14,
        out_specs=anywhere,
        scratch_shapes=[
            pltpu.VMEM((ROWS, COLS, C), BF16),
            pltpu.VMEM((LT, (ROWS + 6) * PITCH, 128), F32),
            pltpu.VMEM((16, LT, 64, 128), F32),
            pltpu.VMEM((7, 7, C), F32),
            *[pltpu.VMEM((C,), F32) for _ in range(7)],
            pltpu.VMEM((HID,), F32),
            pltpu.VMEM((C2,), F32),
            pltpu.VMEM((LT, 49, 8, 128), F32),
            pltpu.VMEM((8, C), F32),
            pltpu.VMEM((1, HID), F32),
            pltpu.VMEM((1, C2), F32),
            pltpu.VMEM((C, HID), BF16),
            pltpu.VMEM((HID, C), BF16),
            pltpu.VMEM((4 * C, C2), BF16),
            pltpu.VMEM((M, C), BF16),
            pltpu.VMEM((M, C), BF16),
            pltpu.VMEM((M, C), BF16),
            pltpu.VMEM((M, C), F32),
            pltpu.VMEM((M, C), F32),
            pltpu.VMEM((2 * HALF, 4 * C), BF16),
            pltpu.VMEM((4, STEPS, 3, HALF, 128), BF16),
            pltpu.VMEM((2, 3, ROWS, C), BF16),
            pltpu.VMEM((2, 3, COLS, C), BF16),
            pltpu.VMEM((2, 3, ROWS, C), BF16),
            pltpu.VMEM((2, 2, 3, 16, C), BF16),
            dma((3,)), dma((3,)), dma((10,)), dma((2,)), dma((2,)), dma((2,)), dma((2,)), dma((2, 2)), dma((2, 2)),
            dma((4, STEPS)), dma((4, STEPS)), dma((STEPS,)),
        ],
        compiler_params=pltpu.CompilerParams(
            collective_id=0, has_side_effects=True, vmem_limit_bytes=56 * 2**20
        ),
    )(
        features, depth_weight, depth_bias, norm_gain, norm_shift, expand_weight, expand_bias,
        reduce_weight, reduce_bias, layer_scale, down_gain, down_shift,
        down_weight.reshape(4 * C, C2), down_bias,
    )
    return pl.pallas_call(
        unpack_kernel,
        grid=(2,),
        out_shape=jax.ShapeDtypeStruct((64, HALF, C2 // 4), BF16),
        in_specs=[pl.BlockSpec((2, STEPS, 3, HALF, 128), lambda i: (i, 0, 0, 0, 0))],
        out_specs=pl.BlockSpec((32, HALF, C2 // 4), lambda i: (i, 0, 0)),
    )(packed)


def solution(mesh):
    in_specs = (P("rows", "cols", None),) + (P(),) * 13
    return jax.shard_map(
        per_device, mesh=mesh, in_specs=in_specs, out_specs=P(None, "cols", "rows"), check_vma=False
    )
```

```python
import jax
import jax.numpy as jnp
from jax import lax
from jax.experimental import pallas as pl
from jax.experimental.pallas import tpu as pltpu
from jax.sharding import PartitionSpec as P

MESH = pl.DeviceIdType.MESH
F32 = jnp.float32
BF16 = jnp.bfloat16

ROWS, COLS, C, HID, C2 = 32, 128, 384, 1536, 768
LT = C // 128
PITCH = 144
LEFT = 8
STEP = 4
STEPS = ROWS // STEP
HALF = COLS // 2
M = STEP * COLS
CHUNKS = 6
HC = HID // CHUNKS


def block_kernel(
    feat, dw_hbm, db, gain, shift, w1_hbm, b1_hbm, w2_hbm, b2, scale, dgain, dshift, wd_hbm, bd_hbm,
    out,
    xin, xp, cs, dw, v0, v1, v2, v3, v4, v5, v6, b1_in, bd_in, wb, pv, b1, bd, w1, w2, wd, nb_next, nb_far, nb_new, nb, acc, acc_done, patches, sbuf,
    cbuf, rowh, colh, corner,
    in_sem, w_sem, p_sem, row_s, row_r, col_s, col_r, cor_s, cor_r, out_s, out_r, own_sem,
):
    r = lax.axis_index("rows")
    c = lax.axis_index("cols")
    nr, nc = 4, lax.axis_size("cols")
    up, down = lax.rem(r + nr - 1, nr), lax.rem(r + 1, nr)
    left, right = lax.rem(c + nc - 1, nc), lax.rem(c + 1, nc)

    spans = [(0, 16), (COLS - 16, 16), (16, COLS - 32)]
    loads = [
        pltpu.make_async_copy(
            feat.at[:, pl.ds(at, size)], xin.at[:, pl.ds(at, size)], in_sem.at[n]
        )
        for n, (at, size) in enumerate(spans)
    ]
    loads += [
        pltpu.make_async_copy(src, dst, w_sem.at[n])
        for n, (src, dst) in enumerate([(w1_hbm, w1), (w2_hbm, w2), (wd_hbm, wd)])
    ]
    vecs = (v0, v1, v2, v3, v4, v5, v6)
    small = list(zip((db, gain, shift, b2, scale, dgain, dshift), vecs))
    small += [(dw_hbm, dw), (b1_hbm, b1_in), (bd_hbm, bd_in)]
    small = [pltpu.make_async_copy(src, dst, p_sem.at[n]) for n, (src, dst) in enumerate(small)]
    for load in loads[:2] + small + loads[2:3]:
        load.start()

    barrier = pltpu.get_barrier_semaphore()
    partners = [(lax.rem(r + j, nr), c) for j in (1, 2, 3)]
    partners += [(r, left), (r, right)]
    for who in partners:
        pl.semaphore_signal(barrier, inc=1, device_id=who, device_id_type=MESH)

    def vec(n, t):
        return pv[pl.ds(n, 1), pl.ds(t * 128, 128)]

    def fill(span):
        at, size = span

        def one(i, carry):
            to = pl.multiple_of((i + 3) * PITCH + LEFT + at, 8)
            for t in range(LT):
                xp[t, pl.ds(to, size), :] = xin[i, pl.ds(at, size), pl.ds(t * 128, 128)].astype(F32)
            return carry

        lax.fori_loop(0, ROWS, one, 0, unroll=4)

    for side in range(2):
        loads[side].wait()
        fill(spans[side])
        for j in range(3):
            at = 3 * PITCH + LEFT + (j if side == 0 else COLS - 3 + j)
            for t in range(LT):
                cbuf[side, j, :, pl.ds(t * 128, 128)] = xp[
                    t, pl.ds(at, ROWS, stride=PITCH), :
                ].astype(BF16)

    def col_copy(side):
        return pltpu.make_async_remote_copy(
            src_ref=cbuf.at[side],
            dst_ref=colh.at[1 - side],
            send_sem=col_s.at[side],
            recv_sem=col_r.at[1 - side],
            device_id=(r, left if side == 0 else right),
            device_id_type=MESH,
        )

    def corner_copy(v, side):
        return pltpu.make_async_remote_copy(
            src_ref=colh.at[side, :, pl.ds(16 * v, 16)],
            dst_ref=corner.at[1 - v, side],
            send_sem=cor_s.at[v, side],
            recv_sem=cor_r.at[1 - v, side],
            device_id=(up if v == 0 else down, c),
            device_id_type=MESH,
        )

    def row_copy(k):
        return pltpu.make_async_remote_copy(
            src_ref=feat.at[pl.ds(0 if k == 0 else ROWS - 3, 3)],
            dst_ref=rowh.at[1 - k],
            send_sem=row_s.at[k],
            recv_sem=row_r.at[1 - k],
            device_id=(up if k == 0 else down, c),
            device_id_type=MESH,
        )

    def send_halo():
        pl.semaphore_wait(barrier, len(partners))
        for side in range(2):
            col_copy(side).start()

        @pl.when(r > 0)
        def _():
            row_copy(0).start()

        @pl.when(r < nr - 1)
        def _():
            row_copy(1).start()

    for load in small:
        load.wait()
    for a in range(7):
        for b in range(7):
            for t in range(LT):
                wb[t, a * 7 + b] = jnp.broadcast_to(
                    dw[a, pl.ds(b, 1), pl.ds(t * 128, 128)], (8, 128)
                )
    for n in range(7):
        pv[pl.ds(n, 1), :] = vecs[n][...].reshape(1, C)
    b1[...] = b1_in[...].reshape(1, HID)
    bd[...] = bd_in[...].reshape(1, C2)

    loads[2].wait()
    for load in loads[3:]:
        load.start()
    fill(spans[2])

    has = [(c > 0).astype(F32), (c < nc - 1).astype(F32)]

    def fill_cols():
        for side in range(2):
            col_copy(1 - side).wait_recv()
            for v in range(2):
                corner_copy(v, side).start()
            for j in range(3):
                at = 3 * PITCH + (LEFT - 3 + j if side == 0 else LEFT + COLS + j)
                for t in range(LT):
                    xp[t, pl.ds(at, ROWS, stride=PITCH), :] = (
                        colh[side, j, :, pl.ds(t * 128, 128)].astype(F32) * has[side]
                    )

    def fill_rows():
        for v in range(2):
            base = 0 if v == 0 else ROWS + 3
            inside = r > 0 if v == 0 else r < nr - 1
            for side in range(2):
                corner_copy(1 - v, side).wait_recv()

            @pl.when(inside)
            def _():
                row_copy(1 - v).wait_recv()
                for i in range(3):
                    for t in range(LT):
                        xp[t, pl.ds((base + i) * PITCH + LEFT, COLS), :] = rowh[
                            v, i, :, pl.ds(t * 128, 128)
                        ].astype(F32)
                for side in range(2):
                    for j in range(3):
                        at = base * PITCH + (LEFT - 3 + j if side == 0 else LEFT + COLS + j)
                        for t in range(LT):
                            piece = (
                                corner[v, side, j, :, pl.ds(t * 128, 128)].astype(F32) * has[side]
                            )
                            for i in range(3):
                                row = (13 if v == 0 else 0) + i
                                xp[t, pl.ds(at + i * PITCH, 1), :] = piece[row : row + 1]

            @pl.when(jnp.logical_not(inside))
            def _():
                for i in range(3):
                    for t in range(LT):
                        xp[t, pl.ds((base + i) * PITCH, PITCH), :] = jnp.zeros((PITCH, 128), F32)

    def norm(x):
        center = jnp.sum(x[0] + x[1] + x[2], axis=-1, keepdims=True) * (1.0 / C)
        x = [v - center for v in x]
        spread = jnp.sum(x[0] * x[0] + x[1] * x[1] + x[2] * x[2], axis=-1, keepdims=True) * (1.0 / C)
        f = lax.rsqrt(spread + 1e-06)
        return [v * f for v in x]

    def conv_block(jb, s, slot, t):
        base = s * STEP * PITCH + jb * 16 + (LEFT - 3)
        total = [[None] * 2 for _ in range(STEP)]
        for a in range(7):
            for i in range(STEP):
                x = [xp[t, pl.ds(base + (i + a) * PITCH + o, 8, stride=2), :] for o in range(8)]
                for b in range(7):
                    w = wb[t, a * 7 + b]
                    for par in range(2):
                        p = x[b + par] * w
                        before = total[i][par]
                        total[i][par] = p if before is None else before + p
        for i in range(STEP):
            for par in range(2):
                at = (i * 2 + par) * 8
                cs[slot, t, at : at + 8, :] = total[i][par]

    def conv_part(jb, s, slot):
        for t in range(LT):
            conv_block(jb, s, slot, t)

    def norm1_part(jb, slot, to):
        y = norm([cs[slot, t] + vec(0, t) for t in range(LT)])
        at = pl.ds(pl.multiple_of(jb * 64, 64), 64)
        for t in range(LT):
            to[at, pl.ds(t * 128, 128)] = (y[t] * vec(1, t) + vec(2, t)).astype(BF16)

    def mlp_part(n):
        at = pl.ds(pl.multiple_of(n * HC, HC), HC)
        z = jnp.dot(nb[...], w1[:, at], preferred_element_type=F32) + b1[:, at]
        h = (z + z * lax.erf(z * 0.7071067811865476)).astype(BF16)
        acc[...] += jnp.dot(h, w2[at, :], preferred_element_type=F32)

    def turn():
        nb[...] = nb_new[...]
        nb_new[...] = nb_far[...]
        nb_far[...] = nb_next[...]
        acc_done[...] = acc[...]
        acc[...] = jnp.zeros_like(acc)

    def norm_part(jb, s):
        at = pl.ds(pl.multiple_of(jb * 64, 64), 64)
        x = []
        for t in range(LT):
            f = jnp.concatenate(
                [
                    xp[t, pl.ds((s * STEP + i + 3) * PITCH + jb * 16 + (LEFT + par), 8, stride=2), :]
                    for i in range(STEP)
                    for par in range(2)
                ],
                axis=0,
            )
            v = f + vec(4, t) * (0.5 * acc_done[at, pl.ds(t * 128, 128)] + vec(3, t))
            x.append(v.astype(BF16).astype(F32))
        y = norm(x)
        for t in range(LT):
            v = y[t] * vec(5, t) + vec(6, t)
            for a in range(2):
                for par in range(2):
                    e = a * 2 + par
                    both = jnp.concatenate([v[e * 8 : e * 8 + 8], v[e * 8 + 32 : e * 8 + 40]], axis=0)
                    patches[
                        pl.ds(pl.multiple_of(jb * 16, 16), 16), pl.ds(e * C + t * 128, 128)
                    ] = both.astype(BF16)

    def down_part(k, s):
        low = lax.broadcasted_iota(jnp.int32, (HALF, 128), 1) < 64
        res = jnp.dot(patches[...], wd[...], preferred_element_type=F32) + bd[...]

        def piece(p, tile):
            return jnp.concatenate(
                [res[q * 16 + p * 8 : q * 16 + p * 8 + 8, tile * 128 : tile * 128 + 128] for q in range(8)],
                axis=0,
            )

        for d in range(4):
            for p in range(2):
                sbuf[d, k, p] = piece(p, (0, 2, 3, 5)[d]).astype(BF16)
        for g in range(2):
            e0, e1 = piece(0, (1, 4)[g]), piece(1, (1, 4)[g])
            sbuf[2 * g, k, 2] = jnp.where(low, e0, pltpu.roll(e1, 64, 1)).astype(BF16)
            sbuf[2 * g + 1, k, 2] = jnp.where(low, pltpu.roll(e0, 64, 1), e1).astype(BF16)
        for d in range(4):
            @pl.when(r != d)
            def _():
                out_copy(d, k, s).start()

            @pl.when(r == d)
            def _():
                own_copy(d, k, s).start()

    def out_copy(d, k, s):
        return pltpu.make_async_remote_copy(
            src_ref=sbuf.at[d, k],
            dst_ref=out.at[r, s],
            send_sem=out_s.at[d, k],
            recv_sem=out_r.at[r, k],
            device_id=(d, c),
            device_id_type=MESH,
        )

    def in_copy(src, k, s):
        return pltpu.make_async_remote_copy(
            src_ref=sbuf.at[src, k],
            dst_ref=out.at[src, s],
            send_sem=out_s.at[src, k],
            recv_sem=out_r.at[src, k],
            device_id=(src, c),
            device_id_type=MESH,
        )

    def own_copy(d, k, s):
        return pltpu.make_async_copy(sbuf.at[d, k], out.at[d, s], own_sem.at[k])

    def rows_of(k):
        return lax.rem(k + 1, STEPS)

    def inner(k):
        def one(n, carry):
            jb = n // 3 + 1
            conv_block(jb, rows_of(k), 8 * k + jb, lax.rem(n, 3))
            return carry

        lax.fori_loop(0, 18, one, 0)

    def outer(k):
        def one(n, carry):
            jb = 7 * (n // 3)
            conv_block(jb, rows_of(k), 8 * k + jb, lax.rem(n, 3))
            return carry

        lax.fori_loop(0, 6, one, 0)

    inner(0)
    send_halo()
    inner(1)
    inner(2)
    for jb in range(1, 7):
        for k, to in enumerate((nb, nb_new, nb_far)):
            norm1_part(jb, 8 * k + jb, to)
    fill_cols()
    for k in range(3):
        outer(k)
    for jb in (0, 7):
        for k, to in enumerate((nb, nb_new, nb_far)):
            norm1_part(jb, 8 * k + jb, to)
    for load in loads[3:]:
        load.wait()
    acc[...] = jnp.zeros_like(acc)
    acc_done[...] = jnp.zeros_like(acc)
    def step(k, carry):
        @pl.when(k == STEPS - 4)
        def _():
            fill_rows()

        s = rows_of(k + 2)
        s_old = rows_of(k + STEPS - 2)

        def part(h, carry2):
            for t in range(LT):
                for q in range(4):
                    conv_block(h * 4 + q, s, q, t)
                mlp_part(h * 3 + t)
                norm_part(h * 4 + t, s_old)
            norm_part(h * 4 + 3, s_old)
            for q in range(4):
                norm1_part(h * 4 + q, q, nb_next)
            return carry2

        lax.fori_loop(0, 2, part, 0)

        @pl.when(k >= 2)
        def _():
            down_part(k - 2, s_old)

        turn()
        return carry

    lax.fori_loop(1, STEPS - 2, step, 0)

    def late(k, carry):
        s_old = rows_of(k - 2)

        def part(h, carry2):
            for q in range(4):
                if q < 3:
                    mlp_part(h * 3 + q)
                norm_part(h * 4 + q, s_old)
            return carry2

        lax.fori_loop(0, 2, part, 0)
        down_part(k - 2, s_old)
        turn()
        return carry

    lax.fori_loop(STEPS - 2, STEPS + 1, late, 0)

    def last(h, carry):
        for q in range(4):
            norm_part(h * 4 + q, rows_of(STEPS - 1))
        return carry

    lax.fori_loop(0, 2, last, 0)
    down_part(STEPS - 1, rows_of(STEPS - 1))

    @pl.when(r > 0)
    def _():
        row_copy(0).wait_send()

    @pl.when(r < nr - 1)
    def _():
        row_copy(1).wait_send()

    for side in range(2):
        col_copy(side).wait_send()
        for v in range(2):
            corner_copy(v, side).wait_send()

    def finish(k, carry):
        s = rows_of(k)
        for d in range(4):
            @pl.when(r != d)
            def _():
                in_copy(d, k, s).wait_recv()
                out_copy(d, k, s).wait_send()

            @pl.when(r == d)
            def _():
                own_copy(d, k, s).wait()

        return carry

    lax.fori_loop(0, STEPS, finish, 0)


def unpack_kernel(packed, out):
    odd = lax.rem(lax.axis_index("rows"), 2)
    parts = [(n, s, p) for n in range(2) for s in range(STEPS) for p in range(2)]

    @pl.when(odd == 0)
    def _():
        for n, s, p in parts:
            tail = packed[n, s, 2][:, p * 64 : (p + 1) * 64]
            out[16 * n + 2 * s + p] = jnp.concatenate([packed[n, s, p], tail], axis=1)

    @pl.when(odd == 1)
    def _():
        for n, s, p in parts:
            head = packed[n, s, 2][:, p * 64 : (p + 1) * 64]
            out[16 * n + 2 * s + p] = jnp.concatenate([head, packed[n, s, p]], axis=1)


def per_device(
    features, depth_weight, depth_bias, norm_gain, norm_shift, expand_weight, expand_bias,
    reduce_weight, reduce_bias, layer_scale, down_gain, down_shift, down_weight, down_bias,
):
    anywhere = pl.BlockSpec(memory_space=pl.ANY)
    dma = pltpu.SemaphoreType.DMA
    packed = pl.pallas_call(
        block_kernel,
        out_shape=jax.ShapeDtypeStruct((4, STEPS, 3, HALF, 128), BF16),
        in_specs=[anywhere] * 14,
        out_specs=anywhere,
        scratch_shapes=[
            pltpu.VMEM((ROWS, COLS, C), BF16),
            pltpu.VMEM((LT, (ROWS + 6) * PITCH, 128), F32),
            pltpu.VMEM((24, LT, 64, 128), F32),
            pltpu.VMEM((7, 7, C), F32),
            *[pltpu.VMEM((C,), F32) for _ in range(7)],
            pltpu.VMEM((HID,), F32),
            pltpu.VMEM((C2,), F32),
            pltpu.VMEM((LT, 49, 8, 128), F32),
            pltpu.VMEM((8, C), F32),
            pltpu.VMEM((1, HID), F32),
            pltpu.VMEM((1, C2), F32),
            pltpu.VMEM((C, HID), BF16),
            pltpu.VMEM((HID, C), BF16),
            pltpu.VMEM((4 * C, C2), BF16),
            pltpu.VMEM((M, C), BF16),
            pltpu.VMEM((M, C), BF16),
            pltpu.VMEM((M, C), BF16),
            pltpu.VMEM((M, C), BF16),
            pltpu.VMEM((M, C), F32),
            pltpu.VMEM((M, C), F32),
            pltpu.VMEM((2 * HALF, 4 * C), BF16),
            pltpu.VMEM((4, STEPS, 3, HALF, 128), BF16),
            pltpu.VMEM((2, 3, ROWS, C), BF16),
            pltpu.VMEM((2, 3, COLS, C), BF16),
            pltpu.VMEM((2, 3, ROWS, C), BF16),
            pltpu.VMEM((2, 2, 3, 16, C), BF16),
            dma((3,)), dma((3,)), dma((10,)), dma((2,)), dma((2,)), dma((2,)), dma((2,)), dma((2, 2)), dma((2, 2)),
            dma((4, STEPS)), dma((4, STEPS)), dma((STEPS,)),
        ],
        compiler_params=pltpu.CompilerParams(
            collective_id=0, has_side_effects=True, vmem_limit_bytes=56 * 2**20
        ),
    )(
        features, depth_weight, depth_bias, norm_gain, norm_shift, expand_weight, expand_bias,
        reduce_weight, reduce_bias, layer_scale, down_gain, down_shift,
        down_weight.reshape(4 * C, C2), down_bias,
    )
    return pl.pallas_call(
        unpack_kernel,
        grid=(2,),
        out_shape=jax.ShapeDtypeStruct((64, HALF, C2 // 4), BF16),
        in_specs=[pl.BlockSpec((2, STEPS, 3, HALF, 128), lambda i: (i, 0, 0, 0, 0))],
        out_specs=pl.BlockSpec((32, HALF, C2 // 4), lambda i: (i, 0, 0)),
    )(packed)


def solution(mesh):
    in_specs = (P("rows", "cols", None),) + (P(),) * 13
    return jax.shard_map(
        per_device, mesh=mesh, in_specs=in_specs, out_specs=P(None, "cols", "rows"), check_vma=False
    )
```
